32 devices in a mesh: ctx: 16 (over z, y, x), fsdp: 2 (over core).
Axes of the slice: x: 2, y: 2, z: 4, core: 2. Of those that a mesh axis runs over, the one named last changes fastest.
Arguments:
- block_input: bfloat16 [2, 2048, 1088], P('fsdp', 'ctx'), may hold values from -6 to 6
- cotangent: bfloat16 [2, 2048, 1088], P('fsdp', 'ctx'), may hold values from -6 to 6
- block_order: int32 [32], replicated, may hold values from 0 to 31, each once
- gain_in: bfloat16 [1088], P('fsdp'), may hold values from 0.099609375 to 1.8984375
- shift_in: bfloat16 [1088], P('fsdp'), may hold values from -3 to 3
- w_qkv: bfloat16 [1088, 3264], P('fsdp'), may hold values from -0.1875 to 0.1875
- qv_bias: bfloat16 [2176], P('fsdp'), may hold values from -3 to 3
- w_out: bfloat16 [1088, 1088], P('fsdp'), may hold values from -3 to 3
- out_bias: bfloat16 [1088], P('fsdp'), may hold values from -3 to 3
- gain_mid: bfloat16 [1088], P('fsdp'), may hold values from 0.099609375 to 1.8984375
- shift_mid: bfloat16 [1088], P('fsdp'), may hold values from -3 to 3
- w_fc: bfloat16 [1088, 4352], P('fsdp'), may hold values from -0.1875 to 0.1875
- fc_bias: bfloat16 [4352], P('fsdp'), may hold values from -3 to 3
- w_down: bfloat16 [1088, 4352], P('fsdp'), may hold values from -0.09375 to 0.09375
- down_bias: bfloat16 [1088], P('fsdp'), may hold values from -3 to 3
Outputs:
- block_output: bfloat16 [2, 2048, 1088], P('fsdp', 'ctx')
- grad_block_input: float32 [2, 2048, 1088], P('fsdp', 'ctx')
- grad_gain_in: float32 [1088], P('fsdp')
- grad_shift_in: float32 [1088], P('fsdp')
- grad_w_qkv: float32 [1088, 3264], P('fsdp', 'ctx')
- grad_qv_bias: float32 [2176], P('fsdp')
- grad_w_out: float32 [1088, 1088], P('fsdp', 'ctx')
- grad_out_bias: float32 [1088], P('fsdp')
- grad_gain_mid: float32 [1088], P('fsdp')
- grad_shift_mid: float32 [1088], P('fsdp')
- grad_w_fc: float32 [1088, 4352], P('fsdp', 'ctx')
- grad_fc_bias: float32 [4352], P('fsdp')
- grad_w_down: float32 [1088, 4352], P('fsdp', 'ctx')
- grad_down_bias: float32 [1088], P('fsdp')
The draws below stay inside these ranges and needn't reach their ends.
Inputs may be any that keep to these rules, and one draw needn't show every extreme that they name: block_order holds each of the 32 blocks of positions exactly once.
All inputs are finite; a program needn't handle non-finite values.
Results may differ from the reference program's by a relative error of at most 0.013.
Values may be sent and summed in bfloat16 or wider, within the bound.
A program may use at most 320 MiB of HBM per device.

```python
import math
import jax
import jax.numpy as jnp
from jax import lax

D = 1088
HEADS = 17
HEAD_DIM = 64
FF = 4352
TOK_DEV = 128
LEN = 2048
SEQS = 2
N_CTX = 16


def steps_of(key, extent, shards, least, largest):
    def one(dim, blocks):
        draws = jax.random.uniform(jax.random.fold_in(jax.random.fold_in(key, 6), dim), (blocks,), jnp.float32, least / len(shards), largest / len(shards))
        return jnp.repeat(jnp.exp(draws), extent[dim] // blocks).reshape((-1,) + (1,) * (len(extent) - dim - 1))

    gain = one(*shards[0])
    for cut in shards[1:]:
        gain = gain * one(*cut)
    return gain


def gaussian(rng, extent, scale, bound, pieces=(), held_as=jnp.bfloat16):
    values = scale * jax.random.normal(rng, extent, jnp.float32)
    if pieces:
        values = values * steps_of(rng, extent, pieces, -0.22, 0.18)
    return jnp.clip(values, -bound, bound).astype(held_as)


def setup_inputs(seed: int = 0) -> dict:
    streams_of = jax.random.split(jax.random.key(seed), 16)
    return {
        "block_input": gaussian(streams_of[0], (SEQS, LEN, D), 1.0, 6.0, ((0, 2), (1, 16))),
        "cotangent": gaussian(streams_of[1], (SEQS, LEN, D), 1.0, 6.0, ((0, 2), (1, 16))),
        "block_order": jax.random.permutation(streams_of[2], 2 * N_CTX).astype(jnp.int32),
        "gain_in": jnp.clip(1.0 + 0.18 * jax.random.normal(streams_of[3], (D,), jnp.float32), 0.099609375, 1.8984375).astype(jnp.bfloat16),
        "shift_in": gaussian(streams_of[4], (D,), 0.5, 3.0, ((0, 2),)),
        "w_qkv": gaussian(streams_of[5], (D, 3 * D), D ** -0.5, 0.1875, ((0, 2),)),
        "qv_bias": gaussian(streams_of[6], (2 * D,), 0.5, 3.0, ((0, 2),)),
        "w_out": gaussian(streams_of[7], (D, D), 4 ** -0.5, 3.0, ((0, 2),)),
        "out_bias": gaussian(streams_of[8], (D,), 0.5, 3.0, ((0, 2),)),
        "gain_mid": jnp.clip(1.0 + 0.18 * jax.random.normal(streams_of[9], (D,), jnp.float32), 0.099609375, 1.8984375).astype(jnp.bfloat16),
        "shift_mid": gaussian(streams_of[10], (D,), 0.5, 3.0, ((0, 2),)),
        "w_fc": gaussian(streams_of[11], (D, FF), D ** -0.5, 0.1875, ((0, 2),)),
        "fc_bias": gaussian(streams_of[12], (FF,), 0.5, 3.0, ((0, 2),)),
        "w_down": gaussian(streams_of[13], (D, FF), FF ** -0.5, 0.09375, ((0, 2),)),
        "down_bias": gaussian(streams_of[14], (D,), 0.5, 3.0, ((0, 2),)),
    }


epsilon = 1e-05
gelu_scale = 0.7978845608028654
gelu_cubic = 0.044715

def layer_norm(inputs, gain_vec, shift_vec):
    average = lax.optimization_barrier(jnp.mean(inputs, axis=-1, keepdims=True))
    centred = inputs - average
    variance = lax.optimization_barrier(jnp.mean(centred * centred, axis=-1, keepdims=True))
    inv_std = lax.rsqrt(variance + epsilon)
    normed = centred * inv_std
    return (normed * gain_vec + shift_vec, normed, inv_std)

def norm_back(upstream, normed, inv_std, gain_vec):
    scaled = upstream * gain_vec
    mean_scaled = lax.optimization_barrier(jnp.mean(scaled, axis=-1, keepdims=True))
    mean_cross = lax.optimization_barrier(jnp.mean(scaled * normed, axis=-1, keepdims=True))
    return inv_std * (scaled - mean_scaled - normed * mean_cross)

def gelu_parts(pre_act):
    inner = gelu_scale * (pre_act + gelu_cubic * pre_act * pre_act * pre_act)
    tangent = jnp.tanh(inner)
    value_act = 0.5 * pre_act * (1.0 + tangent)
    slope = 0.5 * (1.0 + tangent) + 0.5 * pre_act * (1.0 - tangent * tangent) * gelu_scale * (1.0 + 3.0 * gelu_cubic * pre_act * pre_act)
    return (value_act, slope)

def to_bf_wide(values):
    return lax.optimization_barrier(values.astype(jnp.bfloat16)).astype(jnp.float32)

def row_positions(block_order):
    half_block = TOK_DEV // 2
    row_ids = jnp.arange(LEN, dtype=jnp.int32)
    return block_order[row_ids // half_block].astype(jnp.int32) * half_block + row_ids % half_block

def attend_forward(queries, keys, values, positions):
    factor = 1.0 / math.sqrt(HEAD_DIM)
    query_block = min(512, LEN)
    block_count = LEN // query_block
    keys_wide = keys.astype(jnp.float32)
    values_wide = values.astype(jnp.float32)

    def one_block(scan_item):
        query_rows, query_pos = scan_item
        scores = jnp.einsum('qhe,khe->hqk', query_rows.astype(jnp.float32), keys_wide) * factor
        allowed = positions[None, None, :] <= query_pos[None, :, None]
        scores = jnp.where(allowed, scores, -1e+30)
        row_max = lax.optimization_barrier(jnp.max(scores, axis=-1, keepdims=True))
        soft_weights = jnp.where(allowed, jnp.exp(scores - row_max), 0.0)
        row_total = lax.optimization_barrier(jnp.sum(soft_weights, axis=-1, keepdims=True))
        value_sum = jnp.einsum('hqk,khe->qhe', to_bf_wide(soft_weights), values_wide)
        attended = value_sum / jnp.transpose(row_total, (1, 0, 2))
        log_total = jnp.transpose((row_max + jnp.log(row_total))[:, :, 0])
        return (attended, log_total)
    attended, log_rows = lax.map(one_block, (queries.reshape(block_count, query_block, HEADS, HEAD_DIM), positions.reshape(block_count, query_block)))
    return (attended.reshape(LEN, HEADS, HEAD_DIM), log_rows.reshape(LEN, HEADS))

def attend_backward(queries, keys, values, positions, log_rows, grad_heads, delta_rows):
    factor = 1.0 / math.sqrt(HEAD_DIM)
    query_block = min(512, LEN)
    block_count = LEN // query_block
    keys_wide = keys.astype(jnp.float32)
    values_wide = values.astype(jnp.float32)

    def one_block(carried, scan_item):
        grad_key, grad_value = carried
        query_rows, query_pos, log_part, grad_part, delta_part = scan_item
        query_wide = query_rows.astype(jnp.float32)
        grad_wide = grad_part.astype(jnp.float32)
        scores = jnp.einsum('qhe,khe->hqk', query_wide, keys_wide) * factor
        allowed = positions[None, None, :] <= query_pos[None, :, None]
        soft_weights = jnp.where(allowed, jnp.exp(scores - jnp.transpose(log_part)[:, :, None]), 0.0)
        grad_soft = jnp.einsum('qhe,khe->hqk', grad_wide, values_wide)
        grad_score = soft_weights * (grad_soft - jnp.transpose(delta_part)[:, :, None])
        score_bf = to_bf_wide(grad_score)
        weight_bf = to_bf_wide(soft_weights)
        grad_query = jnp.einsum('hqk,khe->qhe', score_bf, keys_wide) * factor
        grad_key = grad_key + jnp.einsum('hqk,qhe->khe', score_bf, query_wide) * factor
        grad_value = grad_value + jnp.einsum('hqk,qhe->khe', weight_bf, grad_wide)
        return ((grad_key, grad_value), grad_query)
    zeros_kv = jnp.zeros((LEN, HEADS, HEAD_DIM), jnp.float32)
    scan_items = (queries.reshape(block_count, query_block, HEADS, HEAD_DIM), positions.reshape(block_count, query_block), log_rows.reshape(block_count, query_block, HEADS), grad_heads.reshape(block_count, query_block, HEADS, HEAD_DIM), delta_rows.reshape(block_count, query_block, HEADS))
    (grad_key, grad_value), grad_query = lax.scan(one_block, (zeros_kv, zeros_kv), scan_items)
    return (grad_query.reshape(LEN, HEADS, HEAD_DIM), grad_key, grad_value)

def one_sequence(inputs, upstream, positions, params):
    gain_in, shift_in, w_qkv, qv_bias, w_out, out_bias, gain_mid, shift_mid, w_fc, fc_bias, w_down, down_bias = params
    wide_in = inputs.astype(jnp.float32)
    hidden_in, normed_in, inv_in = layer_norm(wide_in, gain_in.astype(jnp.float32), shift_in.astype(jnp.float32))
    act_in = hidden_in.astype(jnp.bfloat16)
    bias_full = jnp.concatenate([qv_bias[:D].astype(jnp.float32), jnp.zeros((D,), jnp.float32), qv_bias[D:].astype(jnp.float32)])
    qkv_rows = jnp.dot(act_in, w_qkv, preferred_element_type=jnp.float32) + bias_full
    queries = qkv_rows[:, :D].astype(jnp.bfloat16).reshape(LEN, HEADS, HEAD_DIM)
    keys = qkv_rows[:, D:2 * D].astype(jnp.bfloat16).reshape(LEN, HEADS, HEAD_DIM)
    values = qkv_rows[:, 2 * D:].astype(jnp.bfloat16).reshape(LEN, HEADS, HEAD_DIM)
    attended, log_rows = attend_forward(queries, keys, values, positions)
    attended_bf = attended.reshape(LEN, D).astype(jnp.bfloat16)
    residual = wide_in + jnp.dot(attended_bf, w_out, preferred_element_type=jnp.float32) + out_bias.astype(jnp.float32)
    hidden_mid, normed_mid, inv_mid = layer_norm(residual, gain_mid.astype(jnp.float32), shift_mid.astype(jnp.float32))
    act_mid = hidden_mid.astype(jnp.bfloat16)
    pre_act = jnp.dot(act_mid, w_fc, preferred_element_type=jnp.float32) + fc_bias.astype(jnp.float32)
    value_act, slope = gelu_parts(pre_act)
    act_ff = value_act.astype(jnp.bfloat16)
    result = (residual + jnp.dot(act_ff, w_down.T, preferred_element_type=jnp.float32) + down_bias.astype(jnp.float32)).astype(jnp.bfloat16)
    up_wide = upstream.astype(jnp.float32)
    grad_w_down = jnp.dot(upstream.T, act_ff, preferred_element_type=jnp.float32)
    grad_down_bias = lax.optimization_barrier(jnp.sum(up_wide, axis=0))
    grad_pre = jnp.dot(upstream, w_down, preferred_element_type=jnp.float32) * slope
    grad_fc_bias = lax.optimization_barrier(jnp.sum(grad_pre, axis=0))
    grad_pre_bf = grad_pre.astype(jnp.bfloat16)
    grad_w_fc = jnp.dot(act_mid.T, grad_pre_bf, preferred_element_type=jnp.float32)
    grad_norm_mid = jnp.dot(grad_pre_bf, w_fc.T, preferred_element_type=jnp.float32)
    grad_gain_mid = lax.optimization_barrier(jnp.sum(grad_norm_mid * normed_mid, axis=0))
    grad_shift_mid = lax.optimization_barrier(jnp.sum(grad_norm_mid, axis=0))
    grad_res = up_wide + norm_back(grad_norm_mid, normed_mid, inv_mid, gain_mid.astype(jnp.float32))
    grad_out_bias = lax.optimization_barrier(jnp.sum(grad_res, axis=0))
    grad_res_bf = grad_res.astype(jnp.bfloat16)
    grad_w_out = jnp.dot(attended_bf.T, grad_res_bf, preferred_element_type=jnp.float32)
    grad_heads = jnp.dot(grad_res_bf, w_out.T, preferred_element_type=jnp.float32).astype(jnp.bfloat16).reshape(LEN, HEADS, HEAD_DIM)
    delta_rows = lax.optimization_barrier(jnp.sum(grad_heads.astype(jnp.float32) * attended, axis=-1))
    grad_query, grad_key, grad_value = attend_backward(queries, keys, values, positions, log_rows, grad_heads, delta_rows)
    grad_query = grad_query.reshape(LEN, D)
    grad_value = grad_value.reshape(LEN, D)
    grad_qv_bias = jnp.concatenate([lax.optimization_barrier(jnp.sum(grad_query, axis=0)), lax.optimization_barrier(jnp.sum(grad_value, axis=0))])
    grad_qkv = jnp.concatenate([grad_query, grad_key.reshape(LEN, D), grad_value], axis=1).astype(jnp.bfloat16)
    grad_w_qkv = jnp.dot(act_in.T, grad_qkv, preferred_element_type=jnp.float32)
    grad_norm_in = jnp.dot(grad_qkv, w_qkv.T, preferred_element_type=jnp.float32)
    grad_gain_in = lax.optimization_barrier(jnp.sum(grad_norm_in * normed_in, axis=0))
    grad_shift_in = lax.optimization_barrier(jnp.sum(grad_norm_in, axis=0))
    grad_input = grad_res + norm_back(grad_norm_in, normed_in, inv_in, gain_in.astype(jnp.float32))
    grads = (grad_gain_in, grad_shift_in, grad_w_qkv, grad_qv_bias, grad_w_out, grad_out_bias, grad_gain_mid, grad_shift_mid, grad_w_fc, grad_fc_bias, grad_w_down, grad_down_bias)
    return (result, grad_input, grads)

def reference(block_input, cotangent, block_order, gain_in, shift_in, w_qkv, qv_bias, w_out, out_bias, gain_mid, shift_mid, w_fc, fc_bias, w_down, down_bias):
    positions = row_positions(block_order)
    params = (gain_in, shift_in, w_qkv, qv_bias, w_out, out_bias, gain_mid, shift_mid, w_fc, fc_bias, w_down, down_bias)
    results = []
    grad_inputs = []
    totals = None
    for sequence in range(SEQS):
        result, grad_input, grads = one_sequence(block_input[sequence], cotangent[sequence], positions, params)
        results.append(result)
        grad_inputs.append(grad_input)
        if totals is None:
            totals = grads
        else:
            totals = tuple((total + grad for total, grad in zip(totals, grads)))
    return (jnp.stack(results), jnp.stack(grad_inputs), totals[0], totals[1], totals[2], totals[3], totals[4], totals[5], totals[6], totals[7], totals[8], totals[9], totals[10], totals[11])
```

```python
import functools
import math

import jax
import jax.numpy as jnp
from jax import lax
from jax.experimental import pallas as pl
from jax.experimental.pallas import tpu as pltpu
from jax.sharding import PartitionSpec as P

HEAD_DIM = 64


epsilon = 1e-05
gelu_scale = 0.7978845608028654
gelu_cubic = 0.044715


def layer_norm(inputs, gain_vec, shift_vec):
    average = jnp.mean(inputs, axis=-1, keepdims=True)
    centred = inputs - average
    variance = jnp.mean(centred * centred, axis=-1, keepdims=True)
    inv_std = lax.rsqrt(variance + epsilon)
    normed = centred * inv_std
    return (normed * gain_vec + shift_vec, normed, inv_std)


def norm_back(upstream, normed, inv_std, gain_vec):
    scaled = upstream * gain_vec
    mean_scaled = jnp.mean(scaled, axis=-1, keepdims=True)
    mean_cross = jnp.mean(scaled * normed, axis=-1, keepdims=True)
    return inv_std * (scaled - mean_scaled - normed * mean_cross)


def gelu_parts(pre_act):
    inner = gelu_scale * (pre_act + gelu_cubic * pre_act * pre_act * pre_act)
    tangent = jnp.tanh(inner)
    value_act = 0.5 * pre_act * (1.0 + tangent)
    slope = 0.5 * (1.0 + tangent) + 0.5 * pre_act * (1.0 - tangent * tangent) * gelu_scale * (
        1.0 + 3.0 * gelu_cubic * pre_act * pre_act
    )
    return (value_act, slope)


def block_positions(block_order, first_row, row_count, half_block):
    row_ids = first_row + jnp.arange(row_count, dtype=jnp.int32)
    block_ids = row_ids // half_block
    table_ids = jnp.arange(block_order.shape[0], dtype=jnp.int32)
    one_hot = (block_ids[:, None] == table_ids[None, :]).astype(jnp.int32)
    return jnp.sum(one_hot * block_order[None, :], axis=1) * half_block + row_ids % half_block


def attend_kernel(factor, q_ref, k_ref, v_ref, qpos_ref, kpos_ref, o_ref, lse_ref):
    scores = (
        lax.dot_general(
            q_ref[0], k_ref[0], (((1,), (1,)), ((), ())), preferred_element_type=jnp.float32
        )
        * factor
    )
    allowed = kpos_ref[...] <= qpos_ref[...]
    scores = jnp.where(allowed, scores, -1e30)
    row_max = jnp.max(scores, axis=1, keepdims=True)
    weights = jnp.exp(scores - row_max)
    total = jnp.sum(weights, axis=1, keepdims=True)
    summed = jnp.dot(weights.astype(jnp.bfloat16), v_ref[0], preferred_element_type=jnp.float32)
    o_ref[0] = summed / total
    lse_ref[0] = row_max + jnp.log(total)


def attend_back_kernel(
    factor, q_ref, k_ref, v_ref, do_ref, o_ref, lse_ref, qpos_ref, kpos_ref, dq_ref, dk_ref, dv_ref
):
    rows_q = q_ref[0]
    rows_k = k_ref[0]
    rows_do = do_ref[0]
    contract_last = (((1,), (1,)), ((), ()))
    contract_first = (((0,), (0,)), ((), ()))
    scores = (
        lax.dot_general(rows_q, rows_k, contract_last, preferred_element_type=jnp.float32) * factor
    )
    allowed = kpos_ref[...] <= qpos_ref[...]
    weights = jnp.exp(jnp.where(allowed, scores - lse_ref[0], -1e30))
    delta = jnp.sum(rows_do.astype(jnp.float32) * o_ref[0], axis=1, keepdims=True)
    grad_weights = lax.dot_general(
        rows_do, v_ref[0], contract_last, preferred_element_type=jnp.float32
    )
    grad_scores = (weights * (grad_weights - delta)).astype(jnp.bfloat16)
    dq_ref[0] = jnp.dot(grad_scores, rows_k, preferred_element_type=jnp.float32) * factor
    part_k = (
        lax.dot_general(grad_scores, rows_q, contract_first, preferred_element_type=jnp.float32)
        * factor
    )
    part_v = lax.dot_general(
        weights.astype(jnp.bfloat16), rows_do, contract_first, preferred_element_type=jnp.float32
    )

    @pl.when(pl.program_id(1) == 0)
    def _():
        dk_ref[0] = part_k
        dv_ref[0] = part_v

    @pl.when(pl.program_id(1) > 0)
    def _():
        dk_ref[0] += part_k
        dv_ref[0] += part_v


def attention_specs(q_block, key_count):
    row = pl.BlockSpec((1, q_block, HEAD_DIM), lambda h, i: (h, i, 0))
    stat = pl.BlockSpec((1, q_block, 1), lambda h, i: (h, i, 0))
    key = pl.BlockSpec((1, key_count, HEAD_DIM), lambda h, i: (h, 0, 0))
    qpos = pl.BlockSpec((q_block, 1), lambda h, i: (i, 0))
    kpos = pl.BlockSpec((1, key_count), lambda h, i: (0, 0))
    return row, stat, key, qpos, kpos


def attend(q, k, v, qpos, kpos, factor):
    heads, rows, _ = q.shape
    key_count = k.shape[1]
    q_block = min(rows, 256)
    row, stat, key, qspec, kspec = attention_specs(q_block, key_count)
    return pl.pallas_call(
        functools.partial(attend_kernel, factor),
        grid=(heads, rows // q_block),
        in_specs=[row, key, key, qspec, kspec],
        out_specs=[row, stat],
        out_shape=[
            jax.ShapeDtypeStruct((heads, rows, HEAD_DIM), jnp.float32),
            jax.ShapeDtypeStruct((heads, rows, 1), jnp.float32),
        ],
        compiler_params=pltpu.CompilerParams(vmem_limit_bytes=48 * 1024 * 1024),
        cost_estimate=pl.CostEstimate(
            flops=4 * heads * rows * key_count * HEAD_DIM,
            bytes_accessed=heads * (rows + key_count) * HEAD_DIM * 6,
            transcendentals=heads * rows * key_count,
        ),
    )(q, k, v, qpos[:, None], kpos[None, :])


def attend_back(q, k, v, do, o, lse, qpos, kpos, factor):
    heads, rows, _ = q.shape
    key_count = k.shape[1]
    q_block = min(rows, 256)
    row, stat, key, qspec, kspec = attention_specs(q_block, key_count)
    return pl.pallas_call(
        functools.partial(attend_back_kernel, factor),
        grid=(heads, rows // q_block),
        in_specs=[row, key, key, row, row, stat, qspec, kspec],
        out_specs=[row, key, key],
        out_shape=[
            jax.ShapeDtypeStruct((heads, rows, HEAD_DIM), jnp.float32),
            jax.ShapeDtypeStruct((heads, key_count, HEAD_DIM), jnp.float32),
            jax.ShapeDtypeStruct((heads, key_count, HEAD_DIM), jnp.float32),
        ],
        compiler_params=pltpu.CompilerParams(vmem_limit_bytes=56 * 1024 * 1024),
        cost_estimate=pl.CostEstimate(
            flops=10 * heads * rows * key_count * HEAD_DIM,
            bytes_accessed=heads * (rows + key_count) * HEAD_DIM * 14,
            transcendentals=heads * rows * key_count,
        ),
    )(q, k, v, do, o, lse, qpos[:, None], kpos[None, :])


def to_heads(flat):
    return jnp.transpose(flat.reshape(flat.shape[0], -1, HEAD_DIM), (1, 0, 2))


def from_heads(stacked):
    return jnp.transpose(stacked, (1, 0, 2)).reshape(stacked.shape[1], -1)


def spread(flat, count):
    return jnp.transpose(flat.reshape(flat.shape[0], count, -1), (1, 0, 2))


def unspread(stacked):
    return jnp.transpose(stacked, (1, 0, 2)).reshape(stacked.shape[1], -1)


def exchange(stacked):
    return lax.all_to_all(stacked, "ctx", split_axis=0, concat_axis=0, tiled=True)


def local(
    block_input,
    cotangent,
    block_order,
    gain_in,
    shift_in,
    w_qkv,
    qv_bias,
    w_out,
    out_bias,
    gain_mid,
    shift_mid,
    w_fc,
    fc_bias,
    w_down,
    down_bias,
):
    tokens = block_input.shape[1]
    model_width = block_input.shape[2]
    head_count = model_width // HEAD_DIM
    half_block = tokens // 2
    factor = 1.0 / math.sqrt(HEAD_DIM)
    cycle_count = lax.axis_size("ctx")
    gathered = (
        lax.all_gather(gain_in, "fsdp", axis=0, tiled=True),
        lax.all_gather(shift_in, "fsdp", axis=0, tiled=True),
        lax.all_gather(w_qkv, "fsdp", axis=0, tiled=True),
        lax.all_gather(qv_bias, "fsdp", axis=0, tiled=True),
        lax.all_gather(w_out, "fsdp", axis=0, tiled=True),
        lax.all_gather(out_bias, "fsdp", axis=0, tiled=True),
        lax.all_gather(gain_mid, "fsdp", axis=0, tiled=True),
        lax.all_gather(shift_mid, "fsdp", axis=0, tiled=True),
        lax.all_gather(w_fc, "fsdp", axis=0, tiled=True),
        lax.all_gather(fc_bias, "fsdp", axis=0, tiled=True),
        lax.all_gather(w_down, "fsdp", axis=0, tiled=True),
        lax.all_gather(down_bias, "fsdp", axis=0, tiled=True),
    )
    (
        gain_in_full,
        shift_in_full,
        qkv_full,
        qv_full,
        out_full,
        bias_out_full,
        gain_mid_full,
        shift_mid_full,
        fc_full,
        bias_fc_full,
        down_full,
        bias_down_full,
    ) = gathered
    gain_one = gain_in_full.astype(jnp.float32)
    gain_two = gain_mid_full.astype(jnp.float32)
    device_slot = lax.axis_index("ctx")
    query_pos = block_positions(block_order, device_slot * tokens, tokens, half_block)
    length = cycle_count * tokens
    all_pos = block_positions(block_order, 0, length, half_block)
    owned = head_count // cycle_count
    main_width = owned * cycle_count * HEAD_DIM
    rest_width = model_width - main_width
    own_width = owned * HEAD_DIM

    inputs = block_input.reshape(tokens, model_width)
    wide_in = inputs.astype(jnp.float32)
    hidden_in, normed_in, inv_in = layer_norm(wide_in, gain_one, shift_in_full.astype(jnp.float32))
    act_in = hidden_in.astype(jnp.bfloat16)
    bias_full = jnp.concatenate(
        [
            qv_full[:model_width].astype(jnp.float32),
            jnp.zeros((model_width,), jnp.float32),
            qv_full[model_width:].astype(jnp.float32),
        ]
    )
    qkv_rows = jnp.dot(act_in, qkv_full, preferred_element_type=jnp.float32) + bias_full
    qkv_bf = qkv_rows.astype(jnp.bfloat16)
    thirds = [qkv_bf[:, i * model_width : (i + 1) * model_width] for i in range(3)]
    outgoing = []
    if owned:
        outgoing += [spread(t[:, :main_width], cycle_count) for t in thirds]
    if rest_width:
        outgoing += [
            jnp.broadcast_to(t[None, :, main_width:], (cycle_count, tokens, rest_width))
            for t in thirds[1:]
        ]
    arrived = exchange(jnp.concatenate(outgoing, axis=2)).reshape(length, -1)
    attended_parts = []
    if owned:
        own_q, own_k, own_v = (
            to_heads(arrived[:, i * own_width : (i + 1) * own_width]) for i in range(3)
        )
        own_o, own_lse = attend(own_q, own_k, own_v, all_pos, all_pos, factor)
        back = exchange(from_heads(own_o.astype(jnp.bfloat16)).reshape(cycle_count, tokens, -1))
        attended_parts.append(unspread(back))
    if rest_width:
        rest = arrived[:, 3 * own_width :]
        rest_k, rest_v = to_heads(rest[:, :rest_width]), to_heads(rest[:, rest_width:])
        rest_q = to_heads(thirds[0][:, main_width:])
        rest_o, rest_lse = attend(rest_q, rest_k, rest_v, query_pos, all_pos, factor)
        attended_parts.append(from_heads(rest_o.astype(jnp.bfloat16)))
    attended_bf = jnp.concatenate(attended_parts, axis=1)
    residual = (
        wide_in
        + jnp.dot(attended_bf, out_full, preferred_element_type=jnp.float32)
        + bias_out_full.astype(jnp.float32)
    )
    hidden_mid, normed_mid, inv_mid = layer_norm(
        residual, gain_two, shift_mid_full.astype(jnp.float32)
    )
    act_mid = hidden_mid.astype(jnp.bfloat16)
    pre_act = jnp.dot(act_mid, fc_full, preferred_element_type=jnp.float32) + bias_fc_full.astype(
        jnp.float32
    )
    value_act, slope = gelu_parts(pre_act)
    act_ff = value_act.astype(jnp.bfloat16)
    result = (
        residual
        + jnp.dot(act_ff, down_full.T, preferred_element_type=jnp.float32)
        + bias_down_full.astype(jnp.float32)
    ).astype(jnp.bfloat16)
    qkv_back, out_back, fc_back, down_back = (qkv_full, out_full, fc_full, down_full)
    upstream = cotangent.reshape(tokens, model_width)
    up_wide = upstream.astype(jnp.float32)
    grad_down_bias = jnp.sum(up_wide, axis=0)
    grad_pre = jnp.dot(upstream, down_back, preferred_element_type=jnp.float32) * slope
    grad_fc_bias = jnp.sum(grad_pre, axis=0)
    grad_pre_bf = grad_pre.astype(jnp.bfloat16)
    grad_norm_mid = jnp.dot(grad_pre_bf, fc_back.T, preferred_element_type=jnp.float32)
    grad_gain_mid = jnp.sum(grad_norm_mid * normed_mid, axis=0)
    grad_shift_mid = jnp.sum(grad_norm_mid, axis=0)
    grad_res = up_wide + norm_back(grad_norm_mid, normed_mid, inv_mid, gain_two)
    grad_out_bias = jnp.sum(grad_res, axis=0)
    grad_res_bf = grad_res.astype(jnp.bfloat16)
    grad_heads = jnp.dot(grad_res_bf, out_back.T, preferred_element_type=jnp.float32).astype(
        jnp.bfloat16
    )
    outgoing = []
    if owned:
        own_do = to_heads(exchange(spread(grad_heads[:, :main_width], cycle_count)).reshape(length, -1))
        own_grads = attend_back(
            own_q, own_k, own_v, own_do, own_o, own_lse, all_pos, all_pos, factor
        )
        outgoing += [
            from_heads(g.astype(jnp.bfloat16)).reshape(cycle_count, tokens, -1) for g in own_grads
        ]
    if rest_width:
        rest_dq, rest_dk, rest_dv = attend_back(
            rest_q,
            rest_k,
            rest_v,
            to_heads(grad_heads[:, main_width:]),
            rest_o,
            rest_lse,
            query_pos,
            all_pos,
            factor,
        )
        outgoing += [
            from_heads(g.astype(jnp.bfloat16)).reshape(cycle_count, tokens, -1)
            for g in (rest_dk, rest_dv)
        ]
    arrived = exchange(jnp.concatenate(outgoing, axis=2))
    grads = [[], [], []]
    if owned:
        for i in range(3):
            grads[i].append(unspread(arrived[:, :, i * own_width : (i + 1) * own_width]))
    if rest_width:
        rest = jnp.sum(arrived[:, :, 3 * own_width :].astype(jnp.float32), axis=0)
        grads[0].append(from_heads(rest_dq))
        grads[1].append(rest[:, :rest_width])
        grads[2].append(rest[:, rest_width:])
    grad_query, grad_key, grad_value = (
        jnp.concatenate([p.astype(jnp.bfloat16) for p in parts], axis=1) for parts in grads
    )
    grad_qv_bias = jnp.concatenate(
        [
            jnp.sum(grad_query.astype(jnp.float32), axis=0),
            jnp.sum(grad_value.astype(jnp.float32), axis=0),
        ]
    )
    grad_qkv = jnp.concatenate([grad_query, grad_key, grad_value], axis=1)
    grad_norm_in = jnp.dot(grad_qkv, qkv_back.T, preferred_element_type=jnp.float32)
    grad_gain_in = jnp.sum(grad_norm_in * normed_in, axis=0)
    grad_shift_in = jnp.sum(grad_norm_in, axis=0)
    grad_input = grad_res + norm_back(grad_norm_in, normed_in, inv_in, gain_one)
    column_parts = (
        lax.all_to_all(grad_qkv, "ctx", split_axis=1, concat_axis=0, tiled=True),
        lax.all_to_all(grad_res_bf, "ctx", split_axis=1, concat_axis=0, tiled=True),
        lax.all_to_all(grad_pre_bf, "ctx", split_axis=1, concat_axis=0, tiled=True),
        lax.all_to_all(act_ff, "ctx", split_axis=1, concat_axis=0, tiled=True),
    )
    weight_init = tuple(
        (jnp.zeros((model_width, columns.shape[1]), jnp.float32) for columns in column_parts)
    )
    pieces = (
        lax.all_gather(act_in, "ctx", axis=0, tiled=True),
        lax.all_gather(attended_bf, "ctx", axis=0, tiled=True),
        lax.all_gather(act_mid, "ctx", axis=0, tiled=True),
        lax.all_gather(upstream, "ctx", axis=0, tiled=True),
    )
    updated = []
    for total, piece, columns in zip(weight_init, pieces, column_parts):
        updated.append(jnp.dot(piece.T, columns, preferred_element_type=jnp.float32))
    grad_w_qkv, grad_w_out, grad_w_fc, grad_w_down = tuple(updated)
    vectors = (
        grad_gain_in,
        grad_shift_in,
        grad_qv_bias,
        grad_out_bias,
        grad_gain_mid,
        grad_shift_mid,
        grad_fc_bias,
        grad_down_bias,
    )
    shards = lax.axis_size("fsdp")
    packed = jnp.concatenate([v.reshape(shards, -1) for v in vectors], axis=1)
    packed = lax.psum(packed, ("ctx", "fsdp"))
    packed = lax.dynamic_slice_in_dim(packed, lax.axis_index("fsdp"), 1, axis=0)[0]
    vector_out = []
    offset = 0
    for v in vectors:
        vector_out.append(packed[offset : offset + v.shape[0] // shards])
        offset += v.shape[0] // shards
    summed = tuple(
        lax.psum_scatter(g, "fsdp", scatter_dimension=0, tiled=True)
        for g in (grad_w_qkv, grad_w_out, grad_w_fc, grad_w_down)
    ) + tuple(vector_out)
    return (
        result.reshape(1, tokens, model_width),
        grad_input.reshape(1, tokens, model_width),
        summed[4],
        summed[5],
        summed[0],
        summed[6],
        summed[1],
        summed[7],
        summed[8],
        summed[9],
        summed[2],
        summed[10],
        summed[3],
        summed[11],
    )


def solution(mesh):
    in_specs = (
        P("fsdp", "ctx", None),
        P("fsdp", "ctx", None),
        P(),
        P("fsdp"),
        P("fsdp"),
        P("fsdp", None),
        P("fsdp"),
        P("fsdp", None),
        P("fsdp"),
        P("fsdp"),
        P("fsdp"),
        P("fsdp", None),
        P("fsdp"),
        P("fsdp", None),
        P("fsdp"),
    )
    out_specs = (
        P("fsdp", "ctx", None),
        P("fsdp", "ctx", None),
        P("fsdp"),
        P("fsdp"),
        P("fsdp", "ctx"),
        P("fsdp"),
        P("fsdp", "ctx"),
        P("fsdp"),
        P("fsdp"),
        P("fsdp"),
        P("fsdp", "ctx"),
        P("fsdp"),
        P("fsdp", "ctx"),
        P("fsdp"),
    )
    return jax.shard_map(local, mesh=mesh, in_specs=in_specs, out_specs=out_specs, check_vma=False)
```

```python
import functools
import math

import jax
import jax.numpy as jnp
from jax import lax
from jax.experimental import pallas as pl
from jax.experimental.pallas import tpu as pltpu
from jax.sharding import PartitionSpec as P

HEAD_DIM = 64


epsilon = 1e-05
gelu_scale = 0.7978845608028654
gelu_cubic = 0.044715


def layer_norm(inputs, gain_vec, shift_vec):
    average = jnp.mean(inputs, axis=-1, keepdims=True)
    centred = inputs - average
    variance = jnp.mean(centred * centred, axis=-1, keepdims=True)
    inv_std = lax.rsqrt(variance + epsilon)
    normed = centred * inv_std
    return (normed * gain_vec + shift_vec, normed, inv_std)


def norm_back(upstream, normed, inv_std, gain_vec):
    scaled = upstream * gain_vec
    mean_scaled = jnp.mean(scaled, axis=-1, keepdims=True)
    mean_cross = jnp.mean(scaled * normed, axis=-1, keepdims=True)
    return inv_std * (scaled - mean_scaled - normed * mean_cross)


def gelu_parts(pre_act):
    inner = gelu_scale * (pre_act + gelu_cubic * pre_act * pre_act * pre_act)
    tangent = jnp.tanh(inner)
    value_act = 0.5 * pre_act * (1.0 + tangent)
    slope = 0.5 * (1.0 + tangent) + 0.5 * pre_act * (1.0 - tangent * tangent) * gelu_scale * (
        1.0 + 3.0 * gelu_cubic * pre_act * pre_act
    )
    return (value_act, slope)


def block_positions(block_order, first_row, row_count, half_block):
    row_ids = first_row + jnp.arange(row_count, dtype=jnp.int32)
    block_ids = row_ids // half_block
    table_ids = jnp.arange(block_order.shape[0], dtype=jnp.int32)
    one_hot = (block_ids[:, None] == table_ids[None, :]).astype(jnp.int32)
    return jnp.sum(one_hot * block_order[None, :], axis=1) * half_block + row_ids % half_block


def attend_kernel(factor, q_ref, k_ref, v_ref, qpos_ref, kpos_ref, o_ref, lse_ref):
    scores = (
        lax.dot_general(
            q_ref[0], k_ref[0], (((1,), (1,)), ((), ())), preferred_element_type=jnp.float32
        )
        * factor
    )
    allowed = kpos_ref[...] <= qpos_ref[...]
    scores = jnp.where(allowed, scores, -1e30)
    row_max = jnp.max(scores, axis=1, keepdims=True)
    weights = jnp.exp(scores - row_max)
    total = jnp.sum(weights, axis=1, keepdims=True)
    summed = jnp.dot(weights.astype(jnp.bfloat16), v_ref[0], preferred_element_type=jnp.float32)
    o_ref[0] = summed / total
    lse_ref[0] = row_max + jnp.log(total)


def attend_back_kernel(
    factor, q_ref, k_ref, v_ref, do_ref, o_ref, lse_ref, qpos_ref, kpos_ref, dq_ref, dk_ref, dv_ref
):
    rows_q = q_ref[0]
    rows_k = k_ref[0]
    rows_do = do_ref[0]
    contract_last = (((1,), (1,)), ((), ()))
    contract_first = (((0,), (0,)), ((), ()))
    scores = (
        lax.dot_general(rows_q, rows_k, contract_last, preferred_element_type=jnp.float32) * factor
    )
    allowed = kpos_ref[...] <= qpos_ref[...]
    weights = jnp.exp(jnp.where(allowed, scores - lse_ref[0], -1e30))
    delta = jnp.sum(rows_do.astype(jnp.float32) * o_ref[0], axis=1, keepdims=True)
    grad_weights = lax.dot_general(
        rows_do, v_ref[0], contract_last, preferred_element_type=jnp.float32
    )
    grad_scores = (weights * (grad_weights - delta)).astype(jnp.bfloat16)
    dq_ref[0] = jnp.dot(grad_scores, rows_k, preferred_element_type=jnp.float32) * factor
    part_k = (
        lax.dot_general(grad_scores, rows_q, contract_first, preferred_element_type=jnp.float32)
        * factor
    )
    part_v = lax.dot_general(
        weights.astype(jnp.bfloat16), rows_do, contract_first, preferred_element_type=jnp.float32
    )

    @pl.when(pl.program_id(1) == 0)
    def _():
        dk_ref[0] = part_k
        dv_ref[0] = part_v

    @pl.when(pl.program_id(1) > 0)
    def _():
        dk_ref[0] += part_k
        dv_ref[0] += part_v


def attention_specs(q_block, key_count):
    row = pl.BlockSpec((1, q_block, HEAD_DIM), lambda h, i: (h, i, 0))
    stat = pl.BlockSpec((1, q_block, 1), lambda h, i: (h, i, 0))
    key = pl.BlockSpec((1, key_count, HEAD_DIM), lambda h, i: (h, 0, 0))
    qpos = pl.BlockSpec((q_block, 1), lambda h, i: (i, 0))
    kpos = pl.BlockSpec((1, key_count), lambda h, i: (0, 0))
    return row, stat, key, qpos, kpos


def attend(q, k, v, qpos, kpos, factor):
    heads, rows, _ = q.shape
    key_count = k.shape[1]
    q_block = min(rows, 256)
    row, stat, key, qspec, kspec = attention_specs(q_block, key_count)
    return pl.pallas_call(
        functools.partial(attend_kernel, factor),
        grid=(heads, rows // q_block),
        in_specs=[row, key, key, qspec, kspec],
        out_specs=[row, stat],
        out_shape=[
            jax.ShapeDtypeStruct((heads, rows, HEAD_DIM), jnp.float32),
            jax.ShapeDtypeStruct((heads, rows, 1), jnp.float32),
        ],
        compiler_params=pltpu.CompilerParams(vmem_limit_bytes=48 * 1024 * 1024),
        cost_estimate=pl.CostEstimate(
            flops=4 * heads * rows * key_count * HEAD_DIM,
            bytes_accessed=heads * (rows + key_count) * HEAD_DIM * 6,
            transcendentals=heads * rows * key_count,
        ),
    )(q, k, v, qpos[:, None], kpos[None, :])


def attend_back(q, k, v, do, o, lse, qpos, kpos, factor):
    heads, rows, _ = q.shape
    key_count = k.shape[1]
    q_block = min(rows, 256)
    row, stat, key, qspec, kspec = attention_specs(q_block, key_count)
    return pl.pallas_call(
        functools.partial(attend_back_kernel, factor),
        grid=(heads, rows // q_block),
        in_specs=[row, key, key, row, row, stat, qspec, kspec],
        out_specs=[row, key, key],
        out_shape=[
            jax.ShapeDtypeStruct((heads, rows, HEAD_DIM), jnp.float32),
            jax.ShapeDtypeStruct((heads, key_count, HEAD_DIM), jnp.float32),
            jax.ShapeDtypeStruct((heads, key_count, HEAD_DIM), jnp.float32),
        ],
        compiler_params=pltpu.CompilerParams(vmem_limit_bytes=56 * 1024 * 1024),
        cost_estimate=pl.CostEstimate(
            flops=10 * heads * rows * key_count * HEAD_DIM,
            bytes_accessed=heads * (rows + key_count) * HEAD_DIM * 14,
            transcendentals=heads * rows * key_count,
        ),
    )(q, k, v, do, o, lse, qpos[:, None], kpos[None, :])


def to_heads(flat):
    return jnp.transpose(flat.reshape(flat.shape[0], -1, HEAD_DIM), (1, 0, 2))


def from_heads(stacked):
    return jnp.transpose(stacked, (1, 0, 2)).reshape(stacked.shape[1], -1)


def spread(flat, count):
    return jnp.transpose(flat.reshape(flat.shape[0], count, -1), (1, 0, 2))


def unspread(stacked):
    return jnp.transpose(stacked, (1, 0, 2)).reshape(stacked.shape[1], -1)


def exchange(stacked, groups=None):
    return lax.all_to_all(
        stacked, "ctx", split_axis=0, concat_axis=0, tiled=True, axis_index_groups=groups
    )


def ctx_groups(count):
    inner = 1
    while inner * inner < count and count % (2 * inner) == 0:
        inner *= 2
    outer = count // inner
    along_outer = [[i + inner * o for o in range(outer)] for i in range(inner)]
    along_inner = [[i + inner * o for i in range(inner)] for o in range(outer)]
    return along_outer, along_inner


def sum_shards(whole, wire_type):
    shards = lax.axis_size("fsdp")
    rows = whole.shape[0] // shards
    mine = lax.axis_index("fsdp")
    total = lax.dynamic_slice_in_dim(whole, mine * rows, rows, axis=0)
    for step in range(1, shards):
        target = (mine + step) % shards
        part = lax.dynamic_slice_in_dim(whole, target * rows, rows, axis=0).astype(wire_type)
        moved = lax.ppermute(part, "fsdp", [(i, (i + step) % shards) for i in range(shards)])
        total = total + moved.astype(jnp.float32)
    return total


def local(
    block_input,
    cotangent,
    block_order,
    gain_in,
    shift_in,
    w_qkv,
    qv_bias,
    w_out,
    out_bias,
    gain_mid,
    shift_mid,
    w_fc,
    fc_bias,
    w_down,
    down_bias,
):
    tokens = block_input.shape[1]
    model_width = block_input.shape[2]
    head_count = model_width // HEAD_DIM
    half_block = tokens // 2
    factor = 1.0 / math.sqrt(HEAD_DIM)
    cycle_count = lax.axis_size("ctx")
    gathered = (
        lax.all_gather(gain_in, "fsdp", axis=0, tiled=True),
        lax.all_gather(shift_in, "fsdp", axis=0, tiled=True),
        lax.all_gather(w_qkv, "fsdp", axis=0, tiled=True),
        lax.all_gather(qv_bias, "fsdp", axis=0, tiled=True),
        lax.all_gather(w_out, "fsdp", axis=0, tiled=True),
        lax.all_gather(out_bias, "fsdp", axis=0, tiled=True),
        lax.all_gather(gain_mid, "fsdp", axis=0, tiled=True),
        lax.all_gather(shift_mid, "fsdp", axis=0, tiled=True),
        lax.all_gather(w_fc, "fsdp", axis=0, tiled=True),
        lax.all_gather(fc_bias, "fsdp", axis=0, tiled=True),
        lax.all_gather(w_down, "fsdp", axis=0, tiled=True),
        lax.all_gather(down_bias, "fsdp", axis=0, tiled=True),
    )
    (
        gain_in_full,
        shift_in_full,
        qkv_full,
        qv_full,
        out_full,
        bias_out_full,
        gain_mid_full,
        shift_mid_full,
        fc_full,
        bias_fc_full,
        down_full,
        bias_down_full,
    ) = gathered
    gain_one = gain_in_full.astype(jnp.float32)
    gain_two = gain_mid_full.astype(jnp.float32)
    device_slot = lax.axis_index("ctx")
    query_pos = block_positions(block_order, device_slot * tokens, tokens, half_block)
    length = cycle_count * tokens
    all_pos = block_positions(block_order, 0, length, half_block)
    owned = head_count // cycle_count
    main_width = owned * cycle_count * HEAD_DIM
    rest_width = model_width - main_width
    own_width = owned * HEAD_DIM

    inputs = block_input.reshape(tokens, model_width)
    wide_in = inputs.astype(jnp.float32)
    hidden_in, normed_in, inv_in = layer_norm(wide_in, gain_one, shift_in_full.astype(jnp.float32))
    act_in = hidden_in.astype(jnp.bfloat16)
    bias_full = jnp.concatenate(
        [
            qv_full[:model_width].astype(jnp.float32),
            jnp.zeros((model_width,), jnp.float32),
            qv_full[model_width:].astype(jnp.float32),
        ]
    )
    qkv_rows = jnp.dot(act_in, qkv_full, preferred_element_type=jnp.float32) + bias_full
    qkv_bf = qkv_rows.astype(jnp.bfloat16)
    thirds = [qkv_bf[:, i * model_width : (i + 1) * model_width] for i in range(3)]
    outgoing = []
    if owned:
        outgoing += [spread(t[:, :main_width], cycle_count) for t in thirds]
    if rest_width:
        outgoing += [
            jnp.broadcast_to(t[None, :, main_width:], (cycle_count, tokens, rest_width))
            for t in thirds[1:]
        ]
    arrived = exchange(jnp.concatenate(outgoing, axis=2)).reshape(length, -1)
    attended_parts = []
    if owned:
        own_q, own_k, own_v = (
            to_heads(arrived[:, i * own_width : (i + 1) * own_width]) for i in range(3)
        )
        own_o, own_lse = attend(own_q, own_k, own_v, all_pos, all_pos, factor)
        back = exchange(from_heads(own_o.astype(jnp.bfloat16)).reshape(cycle_count, tokens, -1))
        attended_parts.append(unspread(back))
    if rest_width:
        rest = arrived[:, 3 * own_width :]
        rest_k, rest_v = to_heads(rest[:, :rest_width]), to_heads(rest[:, rest_width:])
        rest_q = to_heads(thirds[0][:, main_width:])
        rest_o, rest_lse = attend(rest_q, rest_k, rest_v, query_pos, all_pos, factor)
        attended_parts.append(from_heads(rest_o.astype(jnp.bfloat16)))
    attended_bf = jnp.concatenate(attended_parts, axis=1)
    residual = (
        wide_in
        + jnp.dot(attended_bf, out_full, preferred_element_type=jnp.float32)
        + bias_out_full.astype(jnp.float32)
    )
    hidden_mid, normed_mid, inv_mid = layer_norm(
        residual, gain_two, shift_mid_full.astype(jnp.float32)
    )
    act_mid = hidden_mid.astype(jnp.bfloat16)
    pre_act = jnp.dot(act_mid, fc_full, preferred_element_type=jnp.float32) + bias_fc_full.astype(
        jnp.float32
    )
    value_act, slope = gelu_parts(pre_act)
    act_ff = value_act.astype(jnp.bfloat16)
    result = (
        residual
        + jnp.dot(act_ff, down_full.T, preferred_element_type=jnp.float32)
        + bias_down_full.astype(jnp.float32)
    ).astype(jnp.bfloat16)
    qkv_back, out_back, fc_back, down_back = (qkv_full, out_full, fc_full, down_full)
    upstream = cotangent.reshape(tokens, model_width)
    up_wide = upstream.astype(jnp.float32)
    grad_down_bias = jnp.sum(up_wide, axis=0)
    grad_pre = jnp.dot(upstream, down_back, preferred_element_type=jnp.float32) * slope
    grad_fc_bias = jnp.sum(grad_pre, axis=0)
    grad_pre_bf = grad_pre.astype(jnp.bfloat16)
    grad_norm_mid = jnp.dot(grad_pre_bf, fc_back.T, preferred_element_type=jnp.float32)
    grad_gain_mid = jnp.sum(grad_norm_mid * normed_mid, axis=0)
    grad_shift_mid = jnp.sum(grad_norm_mid, axis=0)
    grad_res = up_wide + norm_back(grad_norm_mid, normed_mid, inv_mid, gain_two)
    grad_out_bias = jnp.sum(grad_res, axis=0)
    grad_res_bf = grad_res.astype(jnp.bfloat16)
    grad_heads = jnp.dot(grad_res_bf, out_back.T, preferred_element_type=jnp.float32).astype(
        jnp.bfloat16
    )
    outgoing = []
    if owned:
        own_do = to_heads(exchange(spread(grad_heads[:, :main_width], cycle_count)).reshape(length, -1))
        own_grads = attend_back(
            own_q, own_k, own_v, own_do, own_o, own_lse, all_pos, all_pos, factor
        )
        outgoing += [
            from_heads(g.astype(jnp.bfloat16)).reshape(cycle_count, tokens, -1) for g in own_grads
        ]
    if rest_width:
        rest_dq, rest_dk, rest_dv = attend_back(
            rest_q,
            rest_k,
            rest_v,
            to_heads(grad_heads[:, main_width:]),
            rest_o,
            rest_lse,
            query_pos,
            all_pos,
            factor,
        )
        outgoing += [
            from_heads(g.astype(jnp.bfloat16)).reshape(cycle_count, tokens, -1)
            for g in (rest_dk, rest_dv)
        ]
    arrived = exchange(jnp.concatenate(outgoing, axis=2))
    grads = [[], [], []]
    if owned:
        for i in range(3):
            grads[i].append(unspread(arrived[:, :, i * own_width : (i + 1) * own_width]))
    if rest_width:
        rest = jnp.sum(arrived[:, :, 3 * own_width :].astype(jnp.float32), axis=0)
        grads[0].append(from_heads(rest_dq))
        grads[1].append(rest[:, :rest_width])
        grads[2].append(rest[:, rest_width:])
    grad_query, grad_key, grad_value = (
        jnp.concatenate([p.astype(jnp.bfloat16) for p in parts], axis=1) for parts in grads
    )
    grad_qv_bias = jnp.concatenate(
        [
            jnp.sum(grad_query.astype(jnp.float32), axis=0),
            jnp.sum(grad_value.astype(jnp.float32), axis=0),
        ]
    )
    grad_qkv = jnp.concatenate([grad_query, grad_key, grad_value], axis=1)
    grad_norm_in = jnp.dot(grad_qkv, qkv_back.T, preferred_element_type=jnp.float32)
    grad_gain_in = jnp.sum(grad_norm_in * normed_in, axis=0)
    grad_shift_in = jnp.sum(grad_norm_in, axis=0)
    grad_input = grad_res + norm_back(grad_norm_in, normed_in, inv_in, gain_one)
    along_outer, along_inner = ctx_groups(cycle_count)
    outer, inner = len(along_outer[0]), len(along_inner[0])

    def gather_rows(rows):
        return lax.all_gather(rows, "ctx", axis=0, tiled=True, axis_index_groups=along_outer)

    def column_share(parts):
        sent = jnp.concatenate([spread(p, outer) for p in parts], axis=2)
        got = exchange(sent, along_outer).reshape(outer * tokens, -1)
        shares = []
        start = 0
        for p in parts:
            width = p.shape[1] // outer
            shares.append(got[:, start : start + width])
            start += width
        return shares

    def weight_sums(row_parts, column_parts):
        partial = []
        for rows, columns in zip(row_parts, column_share(column_parts)):
            whole = lax.dot_general(
                gather_rows(rows),
                columns,
                (((0,), (0,)), ((), ())),
                preferred_element_type=jnp.float32,
            )
            share = sum_shards(whole, jnp.bfloat16).astype(jnp.bfloat16)
            partial.append(spread(share, inner))
        got = exchange(jnp.concatenate(partial, axis=2), along_inner)
        total = jnp.sum(got.astype(jnp.float32), axis=0)
        sums = []
        start = 0
        for p in partial:
            sums.append(total[:, start : start + p.shape[2]])
            start += p.shape[2]
        return sums

    grad_w_fc, grad_w_down, grad_w_out = weight_sums(
        (act_mid, upstream, attended_bf), (grad_pre_bf, act_ff, grad_res_bf)
    )
    (grad_w_qkv,) = weight_sums((act_in,), (grad_qkv,))
    vectors = (
        grad_gain_in,
        grad_shift_in,
        grad_qv_bias,
        grad_out_bias,
        grad_gain_mid,
        grad_shift_mid,
        grad_fc_bias,
        grad_down_bias,
    )
    shards = lax.axis_size("fsdp")
    packed = jnp.concatenate([v.reshape(shards, -1) for v in vectors], axis=1)
    packed = sum_shards(packed, jnp.float32)
    packed = jnp.sum(lax.all_gather(packed, "ctx", axis=0, tiled=True), axis=0)
    vector_out = []
    offset = 0
    for v in vectors:
        vector_out.append(packed[offset : offset + v.shape[0] // shards])
        offset += v.shape[0] // shards
    summed = (grad_w_qkv, grad_w_out, grad_w_fc, grad_w_down) + tuple(vector_out)
    return (
        result.reshape(1, tokens, model_width),
        grad_input.reshape(1, tokens, model_width),
        summed[4],
        summed[5],
        summed[0],
        summed[6],
        summed[1],
        summed[7],
        summed[8],
        summed[9],
        summed[2],
        summed[10],
        summed[3],
        summed[11],
    )


def solution(mesh):
    in_specs = (
        P("fsdp", "ctx", None),
        P("fsdp", "ctx", None),
        P(),
        P("fsdp"),
        P("fsdp"),
        P("fsdp", None),
        P("fsdp"),
        P("fsdp", None),
        P("fsdp"),
        P("fsdp"),
        P("fsdp"),
        P("fsdp", None),
        P("fsdp"),
        P("fsdp", None),
        P("fsdp"),
    )
    out_specs = (
        P("fsdp", "ctx", None),
        P("fsdp", "ctx", None),
        P("fsdp"),
        P("fsdp"),
        P("fsdp", "ctx"),
        P("fsdp"),
        P("fsdp", "ctx"),
        P("fsdp"),
        P("fsdp"),
        P("fsdp"),
        P("fsdp", "ctx"),
        P("fsdp"),
        P("fsdp", "ctx"),
        P("fsdp"),
    )
    return jax.shard_map(local, mesh=mesh, in_specs=in_specs, out_specs=out_specs, check_vma=False)
```

```python
import functools
import math

import jax
import jax.numpy as jnp
from jax import lax
from jax.experimental import pallas as pl
from jax.experimental.pallas import tpu as pltpu
from jax.sharding import PartitionSpec as P

HEAD_DIM = 64


epsilon = 1e-05
gelu_scale = 0.7978845608028654
gelu_cubic = 0.044715


def layer_norm(inputs, gain_vec, shift_vec):
    average = jnp.mean(inputs, axis=-1, keepdims=True)
    centred = inputs - average
    variance = jnp.mean(centred * centred, axis=-1, keepdims=True)
    inv_std = lax.rsqrt(variance + epsilon)
    normed = centred * inv_std
    return (normed * gain_vec + shift_vec, normed, inv_std)


def norm_back(upstream, normed, inv_std, gain_vec):
    scaled = upstream * gain_vec
    mean_scaled = jnp.mean(scaled, axis=-1, keepdims=True)
    mean_cross = jnp.mean(scaled * normed, axis=-1, keepdims=True)
    return inv_std * (scaled - mean_scaled - normed * mean_cross)


def gelu_parts(pre_act):
    inner = gelu_scale * (pre_act + gelu_cubic * pre_act * pre_act * pre_act)
    tangent = jnp.tanh(inner)
    value_act = 0.5 * pre_act * (1.0 + tangent)
    slope = 0.5 * (1.0 + tangent) + 0.5 * pre_act * (1.0 - tangent * tangent) * gelu_scale * (
        1.0 + 3.0 * gelu_cubic * pre_act * pre_act
    )
    return (value_act, slope)


def block_positions(block_order, first_row, row_count, half_block):
    row_ids = first_row + jnp.arange(row_count, dtype=jnp.int32)
    block_ids = row_ids // half_block
    table_ids = jnp.arange(block_order.shape[0], dtype=jnp.int32)
    one_hot = (block_ids[:, None] == table_ids[None, :]).astype(jnp.int32)
    return jnp.sum(one_hot * block_order[None, :], axis=1) * half_block + row_ids % half_block


def attend_kernel(factor, q_ref, k_ref, v_ref, qpos_ref, kpos_ref, o_ref, lse_ref):
    scores = (
        lax.dot_general(
            q_ref[0], k_ref[0], (((1,), (1,)), ((), ())), preferred_element_type=jnp.float32
        )
        * factor
    )
    allowed = kpos_ref[...] <= qpos_ref[...]
    scores = jnp.where(allowed, scores, -1e30)
    row_max = jnp.max(scores, axis=1, keepdims=True)
    weights = jnp.exp(scores - row_max)
    total = jnp.sum(weights, axis=1, keepdims=True)
    summed = jnp.dot(weights.astype(jnp.bfloat16), v_ref[0], preferred_element_type=jnp.float32)
    o_ref[0] = summed / total
    lse_ref[0] = row_max + jnp.log(total)


def attend_back_kernel(
    factor, q_ref, k_ref, v_ref, do_ref, o_ref, lse_ref, qpos_ref, kpos_ref, dq_ref, dk_ref, dv_ref
):
    rows_q = q_ref[0]
    rows_k = k_ref[0]
    rows_do = do_ref[0]
    contract_last = (((1,), (1,)), ((), ()))
    contract_first = (((0,), (0,)), ((), ()))
    scores = (
        lax.dot_general(rows_q, rows_k, contract_last, preferred_element_type=jnp.float32) * factor
    )
    allowed = kpos_ref[...] <= qpos_ref[...]
    weights = jnp.exp(jnp.where(allowed, scores - lse_ref[0], -1e30))
    delta = jnp.sum(rows_do.astype(jnp.float32) * o_ref[0], axis=1, keepdims=True)
    grad_weights = lax.dot_general(
        rows_do, v_ref[0], contract_last, preferred_element_type=jnp.float32
    )
    grad_scores = (weights * (grad_weights - delta)).astype(jnp.bfloat16)
    dq_ref[0] = jnp.dot(grad_scores, rows_k, preferred_element_type=jnp.float32) * factor
    part_k = (
        lax.dot_general(grad_scores, rows_q, contract_first, preferred_element_type=jnp.float32)
        * factor
    )
    part_v = lax.dot_general(
        weights.astype(jnp.bfloat16), rows_do, contract_first, preferred_element_type=jnp.float32
    )

    @pl.when(pl.program_id(1) == 0)
    def _():
        dk_ref[0] = part_k
        dv_ref[0] = part_v

    @pl.when(pl.program_id(1) > 0)
    def _():
        dk_ref[0] += part_k
        dv_ref[0] += part_v


def attention_specs(q_block, key_count):
    row = pl.BlockSpec((1, q_block, HEAD_DIM), lambda h, i: (h, i, 0))
    stat = pl.BlockSpec((1, q_block, 1), lambda h, i: (h, i, 0))
    key = pl.BlockSpec((1, key_count, HEAD_DIM), lambda h, i: (h, 0, 0))
    qpos = pl.BlockSpec((q_block, 1), lambda h, i: (i, 0))
    kpos = pl.BlockSpec((1, key_count), lambda h, i: (0, 0))
    return row, stat, key, qpos, kpos


def attend(q, k, v, qpos, kpos, factor):
    heads, rows, _ = q.shape
    key_count = k.shape[1]
    q_block = min(rows, 256)
    row, stat, key, qspec, kspec = attention_specs(q_block, key_count)
    return pl.pallas_call(
        functools.partial(attend_kernel, factor),
        grid=(heads, rows // q_block),
        in_specs=[row, key, key, qspec, kspec],
        out_specs=[row, stat],
        out_shape=[
            jax.ShapeDtypeStruct((heads, rows, HEAD_DIM), jnp.float32),
            jax.ShapeDtypeStruct((heads, rows, 1), jnp.float32),
        ],
        compiler_params=pltpu.CompilerParams(vmem_limit_bytes=48 * 1024 * 1024),
        cost_estimate=pl.CostEstimate(
            flops=4 * heads * rows * key_count * HEAD_DIM,
            bytes_accessed=heads * (rows + key_count) * HEAD_DIM * 6,
            transcendentals=heads * rows * key_count,
        ),
    )(q, k, v, qpos[:, None], kpos[None, :])


def attend_back(q, k, v, do, o, lse, qpos, kpos, factor):
    heads, rows, _ = q.shape
    key_count = k.shape[1]
    q_block = min(rows, 256)
    row, stat, key, qspec, kspec = attention_specs(q_block, key_count)
    return pl.pallas_call(
        functools.partial(attend_back_kernel, factor),
        grid=(heads, rows // q_block),
        in_specs=[row, key, key, row, row, stat, qspec, kspec],
        out_specs=[row, key, key],
        out_shape=[
            jax.ShapeDtypeStruct((heads, rows, HEAD_DIM), jnp.float32),
            jax.ShapeDtypeStruct((heads, key_count, HEAD_DIM), jnp.float32),
            jax.ShapeDtypeStruct((heads, key_count, HEAD_DIM), jnp.float32),
        ],
        compiler_params=pltpu.CompilerParams(vmem_limit_bytes=56 * 1024 * 1024),
        cost_estimate=pl.CostEstimate(
            flops=10 * heads * rows * key_count * HEAD_DIM,
            bytes_accessed=heads * (rows + key_count) * HEAD_DIM * 14,
            transcendentals=heads * rows * key_count,
        ),
    )(q, k, v, do, o, lse, qpos[:, None], kpos[None, :])


def to_heads(flat):
    return jnp.transpose(flat.reshape(flat.shape[0], -1, HEAD_DIM), (1, 0, 2))


def from_heads(stacked):
    return jnp.transpose(stacked, (1, 0, 2)).reshape(stacked.shape[1], -1)


def spread(flat, count):
    return jnp.transpose(flat.reshape(flat.shape[0], count, -1), (1, 0, 2))


def unspread(stacked):
    return jnp.transpose(stacked, (1, 0, 2)).reshape(stacked.shape[1], -1)


def exchange(stacked, groups=None):
    return lax.all_to_all(
        stacked, "ctx", split_axis=0, concat_axis=0, tiled=True, axis_index_groups=groups
    )


def ctx_groups(count):
    inner = 1
    while inner * inner < count and count % (2 * inner) == 0:
        inner *= 2
    outer = count // inner
    along_outer = [[i + inner * o for o in range(outer)] for i in range(inner)]
    along_inner = [[i + inner * o for i in range(inner)] for o in range(outer)]
    return along_outer, along_inner


def sum_shards(whole, wire_type):
    shards = lax.axis_size("fsdp")
    rows = whole.shape[0] // shards
    mine = lax.axis_index("fsdp")
    total = lax.dynamic_slice_in_dim(whole, mine * rows, rows, axis=0)
    for step in range(1, shards):
        target = (mine + step) % shards
        part = lax.dynamic_slice_in_dim(whole, target * rows, rows, axis=0).astype(wire_type)
        moved = lax.ppermute(part, "fsdp", [(i, (i + step) % shards) for i in range(shards)])
        total = total + moved.astype(jnp.float32)
    return total


def local(
    block_input,
    cotangent,
    block_order,
    gain_in,
    shift_in,
    w_qkv,
    qv_bias,
    w_out,
    out_bias,
    gain_mid,
    shift_mid,
    w_fc,
    fc_bias,
    w_down,
    down_bias,
):
    tokens = block_input.shape[1]
    model_width = block_input.shape[2]
    head_count = model_width // HEAD_DIM
    half_block = tokens // 2
    factor = 1.0 / math.sqrt(HEAD_DIM)
    cycle_count = lax.axis_size("ctx")
    gathered = (
        lax.all_gather(gain_in, "fsdp", axis=0, tiled=True),
        lax.all_gather(shift_in, "fsdp", axis=0, tiled=True),
        lax.all_gather(w_qkv, "fsdp", axis=0, tiled=True),
        lax.all_gather(qv_bias, "fsdp", axis=0, tiled=True),
        lax.all_gather(w_out, "fsdp", axis=0, tiled=True),
        lax.all_gather(out_bias, "fsdp", axis=0, tiled=True),
        lax.all_gather(gain_mid, "fsdp", axis=0, tiled=True),
        lax.all_gather(shift_mid, "fsdp", axis=0, tiled=True),
        lax.all_gather(w_fc, "fsdp", axis=0, tiled=True),
        lax.all_gather(fc_bias, "fsdp", axis=0, tiled=True),
        lax.all_gather(w_down, "fsdp", axis=0, tiled=True),
        lax.all_gather(down_bias, "fsdp", axis=0, tiled=True),
    )
    (
        gain_in_full,
        shift_in_full,
        qkv_full,
        qv_full,
        out_full,
        bias_out_full,
        gain_mid_full,
        shift_mid_full,
        fc_full,
        bias_fc_full,
        down_full,
        bias_down_full,
    ) = gathered
    gain_one = gain_in_full.astype(jnp.float32)
    gain_two = gain_mid_full.astype(jnp.float32)
    device_slot = lax.axis_index("ctx")
    query_pos = block_positions(block_order, device_slot * tokens, tokens, half_block)
    length = cycle_count * tokens
    all_pos = block_positions(block_order, 0, length, half_block)
    owned = head_count // cycle_count
    main_width = owned * cycle_count * HEAD_DIM
    rest_width = model_width - main_width
    own_width = owned * HEAD_DIM

    inputs = block_input.reshape(tokens, model_width)
    wide_in = inputs.astype(jnp.float32)
    hidden_in, normed_in, inv_in = layer_norm(wide_in, gain_one, shift_in_full.astype(jnp.float32))
    act_in = hidden_in.astype(jnp.bfloat16)
    bias_full = jnp.concatenate(
        [
            qv_full[:model_width].astype(jnp.float32),
            jnp.zeros((model_width,), jnp.float32),
            qv_full[model_width:].astype(jnp.float32),
        ]
    )
    qkv_rows = jnp.dot(act_in, qkv_full, preferred_element_type=jnp.float32) + bias_full
    qkv_bf = qkv_rows.astype(jnp.bfloat16)
    thirds = [qkv_bf[:, i * model_width : (i + 1) * model_width] for i in range(3)]
    outgoing = []
    if owned:
        outgoing += [spread(t[:, :main_width], cycle_count) for t in thirds]
    if rest_width:
        outgoing += [
            jnp.broadcast_to(t[None, :, main_width:], (cycle_count, tokens, rest_width))
            for t in thirds[1:]
        ]
    arrived = exchange(jnp.concatenate(outgoing, axis=2)).reshape(length, -1)
    attended_parts = []
    if owned:
        own_q, own_k, own_v = (
            to_heads(arrived[:, i * own_width : (i + 1) * own_width]) for i in range(3)
        )
        own_o, own_lse = attend(own_q, own_k, own_v, all_pos, all_pos, factor)
        back = exchange(from_heads(own_o.astype(jnp.bfloat16)).reshape(cycle_count, tokens, -1))
        attended_parts.append(unspread(back))
    if rest_width:
        rest = arrived[:, 3 * own_width :]
        rest_k, rest_v = to_heads(rest[:, :rest_width]), to_heads(rest[:, rest_width:])
        rest_q = to_heads(thirds[0][:, main_width:])
        rest_o, rest_lse = attend(rest_q, rest_k, rest_v, query_pos, all_pos, factor)
        attended_parts.append(from_heads(rest_o.astype(jnp.bfloat16)))
    attended_bf = jnp.concatenate(attended_parts, axis=1)
    residual = (
        wide_in
        + jnp.dot(attended_bf, out_full, preferred_element_type=jnp.float32)
        + bias_out_full.astype(jnp.float32)
    )
    hidden_mid, normed_mid, inv_mid = layer_norm(
        residual, gain_two, shift_mid_full.astype(jnp.float32)
    )
    act_mid = hidden_mid.astype(jnp.bfloat16)
    pre_act = jnp.dot(act_mid, fc_full, preferred_element_type=jnp.float32) + bias_fc_full.astype(
        jnp.float32
    )
    value_act, slope = gelu_parts(pre_act)
    act_ff = value_act.astype(jnp.bfloat16)
    result = (
        residual
        + jnp.dot(act_ff, down_full.T, preferred_element_type=jnp.float32)
        + bias_down_full.astype(jnp.float32)
    ).astype(jnp.bfloat16)
    qkv_back, out_back, fc_back, down_back = (qkv_full, out_full, fc_full, down_full)
    upstream = cotangent.reshape(tokens, model_width)
    up_wide = upstream.astype(jnp.float32)
    grad_down_bias = jnp.sum(up_wide, axis=0)
    grad_pre = jnp.dot(upstream, down_back, preferred_element_type=jnp.float32) * slope
    grad_fc_bias = jnp.sum(grad_pre, axis=0)
    grad_pre_bf = grad_pre.astype(jnp.bfloat16)
    grad_norm_mid = jnp.dot(grad_pre_bf, fc_back.T, preferred_element_type=jnp.float32)
    grad_gain_mid = jnp.sum(grad_norm_mid * normed_mid, axis=0)
    grad_shift_mid = jnp.sum(grad_norm_mid, axis=0)
    grad_res = up_wide + norm_back(grad_norm_mid, normed_mid, inv_mid, gain_two)
    grad_out_bias = jnp.sum(grad_res, axis=0)
    grad_res_bf = grad_res.astype(jnp.bfloat16)
    along_outer, along_inner = ctx_groups(cycle_count)
    outer, inner = len(along_outer[0]), len(along_inner[0])

    def gather_rows(rows):
        return lax.all_gather(rows, "ctx", axis=0, tiled=True, axis_index_groups=along_outer)

    def column_share(parts):
        sent = jnp.concatenate([spread(p, outer) for p in parts], axis=2)
        got = exchange(sent, along_outer).reshape(outer * tokens, -1)
        shares = []
        start = 0
        for p in parts:
            width = p.shape[1] // outer
            shares.append(got[:, start : start + width])
            start += width
        return shares

    row_shares = [gather_rows(rows) for rows in (act_mid, upstream, attended_bf)]
    column_shares = column_share((grad_pre_bf, act_ff, grad_res_bf))
    grad_heads = jnp.dot(grad_res_bf, out_back.T, preferred_element_type=jnp.float32).astype(
        jnp.bfloat16
    )
    outgoing = []
    if owned:
        own_do = to_heads(exchange(spread(grad_heads[:, :main_width], cycle_count)).reshape(length, -1))
        own_grads = attend_back(
            own_q, own_k, own_v, own_do, own_o, own_lse, all_pos, all_pos, factor
        )
        outgoing += [
            from_heads(g.astype(jnp.bfloat16)).reshape(cycle_count, tokens, -1) for g in own_grads
        ]
    if rest_width:
        rest_dq, rest_dk, rest_dv = attend_back(
            rest_q,
            rest_k,
            rest_v,
            to_heads(grad_heads[:, main_width:]),
            rest_o,
            rest_lse,
            query_pos,
            all_pos,
            factor,
        )
        outgoing += [
            from_heads(g.astype(jnp.bfloat16)).reshape(cycle_count, tokens, -1)
            for g in (rest_dk, rest_dv)
        ]
    outgoing, row_shares, column_shares = lax.optimization_barrier(
        (outgoing, row_shares, column_shares)
    )
    arrived = exchange(jnp.concatenate(outgoing, axis=2))
    grads = [[], [], []]
    if owned:
        for i in range(3):
            grads[i].append(unspread(arrived[:, :, i * own_width : (i + 1) * own_width]))
    if rest_width:
        rest = jnp.sum(arrived[:, :, 3 * own_width :].astype(jnp.float32), axis=0)
        grads[0].append(from_heads(rest_dq))
        grads[1].append(rest[:, :rest_width])
        grads[2].append(rest[:, rest_width:])
    grad_query, grad_key, grad_value = (
        jnp.concatenate([p.astype(jnp.bfloat16) for p in parts], axis=1) for parts in grads
    )
    grad_qv_bias = jnp.concatenate(
        [
            jnp.sum(grad_query.astype(jnp.float32), axis=0),
            jnp.sum(grad_value.astype(jnp.float32), axis=0),
        ]
    )
    grad_qkv = jnp.concatenate([grad_query, grad_key, grad_value], axis=1)
    grad_norm_in = jnp.dot(grad_qkv, qkv_back.T, preferred_element_type=jnp.float32)
    grad_gain_in = jnp.sum(grad_norm_in * normed_in, axis=0)
    grad_shift_in = jnp.sum(grad_norm_in, axis=0)
    grad_input = grad_res + norm_back(grad_norm_in, normed_in, inv_in, gain_one)
    def weight_sums(row_shares, column_shares):
        partial = []
        for rows, columns in zip(row_shares, column_shares):
            whole = lax.dot_general(
                rows,
                columns,
                (((0,), (0,)), ((), ())),
                preferred_element_type=jnp.float32,
            )
            share = sum_shards(whole, jnp.bfloat16).astype(jnp.bfloat16)
            partial.append(spread(share, inner))
        got = exchange(jnp.concatenate(partial, axis=2), along_inner)
        total = jnp.sum(got.astype(jnp.float32), axis=0)
        sums = []
        start = 0
        for p in partial:
            sums.append(total[:, start : start + p.shape[2]])
            start += p.shape[2]
        return sums

    grad_w_fc, grad_w_down, grad_w_out = weight_sums(row_shares, column_shares)
    (grad_w_qkv,) = weight_sums([gather_rows(act_in)], column_share((grad_qkv,)))
    vectors = (
        grad_gain_in,
        grad_shift_in,
        grad_qv_bias,
        grad_out_bias,
        grad_gain_mid,
        grad_shift_mid,
        grad_fc_bias,
        grad_down_bias,
    )
    shards = lax.axis_size("fsdp")
    packed = jnp.concatenate([v.reshape(shards, -1) for v in vectors], axis=1)
    packed = sum_shards(packed, jnp.float32)
    packed = exchange(jnp.broadcast_to(packed[None], (cycle_count,) + packed.shape))
    packed = jnp.sum(packed, axis=(0, 1))
    vector_out = []
    offset = 0
    for v in vectors:
        vector_out.append(packed[offset : offset + v.shape[0] // shards])
        offset += v.shape[0] // shards
    summed = (grad_w_qkv, grad_w_out, grad_w_fc, grad_w_down) + tuple(vector_out)
    return (
        result.reshape(1, tokens, model_width),
        grad_input.reshape(1, tokens, model_width),
        summed[4],
        summed[5],
        summed[0],
        summed[6],
        summed[1],
        summed[7],
        summed[8],
        summed[9],
        summed[2],
        summed[10],
        summed[3],
        summed[11],
    )


def solution(mesh):
    in_specs = (
        P("fsdp", "ctx", None),
        P("fsdp", "ctx", None),
        P(),
        P("fsdp"),
        P("fsdp"),
        P("fsdp", None),
        P("fsdp"),
        P("fsdp", None),
        P("fsdp"),
        P("fsdp"),
        P("fsdp"),
        P("fsdp", None),
        P("fsdp"),
        P("fsdp", None),
        P("fsdp"),
    )
    out_specs = (
        P("fsdp", "ctx", None),
        P("fsdp", "ctx", None),
        P("fsdp"),
        P("fsdp"),
        P("fsdp", "ctx"),
        P("fsdp"),
        P("fsdp", "ctx"),
        P("fsdp"),
        P("fsdp"),
        P("fsdp"),
        P("fsdp", "ctx"),
        P("fsdp"),
        P("fsdp", "ctx"),
        P("fsdp"),
    )
    return jax.shard_map(local, mesh=mesh, in_specs=in_specs, out_specs=out_specs, check_vma=False)
```
